512 devices in a mesh: wide: 32 (over z, y_hi, core), narrow: 16 (over y_lo, x).
Axes of the slice: x: 4, y: 8 (y_hi: 2, y_lo: 4; y = y_hi * 4 + y_lo), z: 8, core: 2. Of those that a mesh axis runs over, the one named last changes fastest.
Arguments:
- packet_prev: float32 [64, 512, 16, 128], P('wide', None, 'narrow'), may hold values from -6 to 6
- packet_curr: float32 [64, 512, 16, 128], P('wide', None, 'narrow'), may hold values from -6 to 6
- potential: float32 [64, 512, 16, 128], P('wide', None, 'narrow'), may hold values from -0.6 to 0.6
- damping: float32 [64, 32], P('wide'), may hold values from 0.5 to 1
- kinetic_radial: float32 [64, 64], replicated, may hold values from -0.5 to 0.5, as said below
- kinetic_bond: float32 [32, 32], replicated, may hold values from -0.5 to 0.5, as said below
- kinetic_bend: float32 [16, 16], replicated, may hold values from -0.5 to 0.5, as said below
- kinetic_twist: float32 [16, 16], replicated, may hold values from -0.5 to 0.5, as said below
- kinetic_torsion: float32 [16, 16], replicated, may hold values from -0.5 to 0.5, as said below
- kinetic_umbrella: float32 [8, 8], replicated, may hold values from -0.5 to 0.5, as said below
Outputs:
- packet_next: float32 [64, 512, 16, 128], P('wide', None, 'narrow')
- packet_last: float32 [64, 512, 16, 128], P('wide', None, 'narrow')
The draws below stay inside these ranges and needn't reach their ends.
Inputs may be any that keep to these rules, and one draw needn't show every extreme that they name: `kinetic_radial`: symmetric. `kinetic_bond`: symmetric. `kinetic_bend`: symmetric. `kinetic_twist`: symmetric. `kinetic_torsion`: symmetric. `kinetic_umbrella`: symmetric.
All inputs are finite; a program needn't handle non-finite values.
Results may differ from the reference program's by a relative error of at most 0.0001.
Values sent between devices are 32-bit elements; how exact they have to be, the bound alone decides.
No kernel may reach another device: no remote copies, remote signals or barrier semaphores. Data moves between devices by JAX's collectives and lax.ppermute only.
A program may use at most 64 MiB of HBM per device.

```python
import math
import jax
import jax.numpy as jnp
from jax import lax

NR = 64
NRR = 32
NTH = 16
NCHI = 16
NPHI = 16
NRHO = 8


def symmetric_kinetic(raw, key, order):
    diagonal = jax.random.uniform(key, (order,), jnp.float32, 0.02, 0.12)
    return (raw + raw.T) * (0.05 / math.sqrt(order)) + jnp.diag(diagonal)


def draw_kinetic_radial(key, part):
    key = jax.random.fold_in(key, 11)
    raw = jax.random.truncated_normal(key, -3.0, 3.0, (NR, NR), jnp.float32)
    return symmetric_kinetic(raw, jax.random.fold_in(key, 99), NR)


def draw_kinetic_bond(key, part):
    key = jax.random.fold_in(key, 12)
    raw = jax.random.truncated_normal(key, -3.0, 3.0, (NRR, NRR), jnp.float32)
    return symmetric_kinetic(raw, jax.random.fold_in(key, 99), NRR)


def draw_kinetic_bend(key, part):
    key = jax.random.fold_in(key, 13)
    raw = jax.random.truncated_normal(key, -3.0, 3.0, (NTH, NTH), jnp.float32)
    return symmetric_kinetic(raw, jax.random.fold_in(key, 99), NTH)


def draw_kinetic_twist(key, part):
    key = jax.random.fold_in(key, 14)
    raw = jax.random.truncated_normal(key, -3.0, 3.0, (NCHI, NCHI), jnp.float32)
    return symmetric_kinetic(raw, jax.random.fold_in(key, 99), NCHI)


def draw_kinetic_torsion(key, part):
    key = jax.random.fold_in(key, 15)
    raw = jax.random.truncated_normal(key, -3.0, 3.0, (NPHI, NPHI), jnp.float32)
    return symmetric_kinetic(raw, jax.random.fold_in(key, 99), NPHI)


def draw_kinetic_umbrella(key, part):
    key = jax.random.fold_in(key, 16)
    raw = jax.random.truncated_normal(key, -3.0, 3.0, (NRHO, NRHO), jnp.float32)
    return symmetric_kinetic(raw, jax.random.fold_in(key, 99), NRHO)


def block_scale(own_key, shape, pieces, low, high):
    factor_of = 1.0
    for axis_at, parts in pieces:
        steps = jax.random.uniform(jax.random.fold_in(jax.random.fold_in(own_key, 6), axis_at), (parts,), jnp.float32, low / len(pieces), high / len(pieces))
        factor_of = factor_of * jnp.repeat(jnp.exp(steps), shape[axis_at] // parts).reshape((-1,) + (1,) * (len(shape) - 1 - axis_at))
    return factor_of


def centred(key, extent, scale, bound, pieces=(), dtype=jnp.bfloat16):
    drawn = jax.random.normal(key, extent, jnp.float32) * scale
    if len(pieces) > 0:
        drawn = block_scale(key, extent, pieces, -0.22, 0.18) * drawn
    return jnp.clip(drawn, min=-bound, max=bound).astype(dtype)


def setup_inputs(seed: int = 0) -> dict:
    key_of = jax.random.split(jax.random.key(seed), 11)
    return {
        "packet_prev": centred(key_of[0], (NR, NRR * NTH, NCHI, NPHI * NRHO), 1.0, 6.0, ((0, 32), (2, 16)), jnp.float32),
        "packet_curr": centred(key_of[1], (NR, NRR * NTH, NCHI, NPHI * NRHO), 1.0, 6.0, ((0, 32), (2, 16)), jnp.float32),
        "potential": jnp.clip(jax.random.uniform(key_of[2], (NR, NRR * NTH, NCHI, NPHI * NRHO), jnp.float32, -0.6, 0.6) * block_scale(key_of[2], (NR, NRR * NTH, NCHI, NPHI * NRHO), ((0, 32), (2, 16)), -0.4, 0.0), -0.6, 0.6),
        "damping": jnp.clip(0.5 + 0.5 * jax.random.uniform(key_of[3], (NR, NRR), jnp.float32) ** block_scale(key_of[3], (NR, NRR), ((0, 32),), -0.2, 0.2), 0.5, 1.0),
        "kinetic_radial": draw_kinetic_radial(jax.random.fold_in(key_of[10], 71), 0),
        "kinetic_bond": draw_kinetic_bond(jax.random.fold_in(key_of[10], 71), 0),
        "kinetic_bend": draw_kinetic_bend(jax.random.fold_in(key_of[10], 71), 0),
        "kinetic_twist": draw_kinetic_twist(jax.random.fold_in(key_of[10], 71), 0),
        "kinetic_torsion": draw_kinetic_torsion(jax.random.fold_in(key_of[10], 71), 0),
        "kinetic_umbrella": draw_kinetic_umbrella(jax.random.fold_in(key_of[10], 71), 0),
    }


def kinetic_apply(grid, matrix, axis):
    moved = jnp.tensordot(matrix, grid, axes=((1,), (axis,)), precision=lax.Precision.HIGHEST)
    return jnp.moveaxis(moved, 0, axis)


def hamiltonian(packet, potential, matrices):
    grid = packet.reshape(NR, NRR, NTH, NCHI, NPHI, NRHO)
    total = (potential * packet).reshape(NR, NRR, NTH, NCHI, NPHI, NRHO)
    for axis in range(6):
        total = total + kinetic_apply(grid, matrices[axis], axis)
    return total.reshape(NR, NRR * NTH, NCHI, NPHI * NRHO)


def reference(packet_prev, packet_curr, potential, damping, kinetic_radial, kinetic_bond, kinetic_bend, kinetic_twist, kinetic_torsion, kinetic_umbrella):
    matrices = (kinetic_radial, kinetic_bond, kinetic_bend, kinetic_twist, kinetic_torsion, kinetic_umbrella)
    damping_full = jnp.broadcast_to(damping[:, :, None], (NR, NRR, NTH)).reshape(NR, NRR * NTH)[:, :, None, None]
    next_term = damping_full * (2.0 * hamiltonian(packet_curr, potential, matrices) - damping_full * packet_prev)
    last_term = damping_full * (2.0 * hamiltonian(next_term, potential, matrices) - damping_full * packet_curr)
    return next_term, last_term
```

```python
import jax
import jax.numpy as jnp
from jax import lax
from jax.experimental import pallas as pl
from jax.experimental.pallas import tpu as pltpu
from jax.sharding import PartitionSpec as P

AXES = ("narrow", "wide")
F32 = jnp.float32
BF16 = jnp.bfloat16


def exact_dot(left, right):
    return jnp.dot(left, right, precision=lax.Precision.HIGHEST, preferred_element_type=F32)


def dot(left, right):
    return jnp.dot(left, right, preferred_element_type=F32)


def split(value):
    high = value.astype(BF16)
    return high, (value - high.astype(F32)).astype(BF16)


def iota(shape, axis):
    return lax.broadcasted_iota(jnp.int32, shape, axis)


def ones_where(condition):
    return jnp.where(condition, 1.0, 0.0).astype(F32)


def build_inner(bond_ref, bend_ref, high_ref, low_ref):
    bonds, bends = bond_ref.shape[0], bend_ref.shape[0]
    size = bonds * bends
    spread_bond = exact_dot(bond_ref[...], ones_where(iota((bonds, size), 0) == iota((bonds, size), 1) // bends))
    spread_bend = exact_dot(bend_ref[...], ones_where(iota((bends, size), 0) == iota((bends, size), 1) % bends))
    same_bend = iota((bends, size), 0) == iota((bends, size), 1) % bends
    bond_of = iota((bends, size), 1) // bends
    for bond in range(bonds):
        row = jnp.broadcast_to(spread_bond[bond : bond + 1, :], (bends, size))
        block = jnp.where(same_bend, row, 0.0) + jnp.where(bond_of == bond, spread_bend, 0.0)
        high, low = split(block)
        high_ref[pl.ds(bond * bends, bends), :] = high
        low_ref[pl.ds(bond * bends, bends), :] = low


def build_outer(torsion_ref, umbrella_ref):
    torsions, umbrellas = torsion_ref.shape[0], umbrella_ref.shape[0]
    size = torsions * umbrellas
    spread = ones_where(iota((torsions, size), 0) == iota((torsions, size), 1) // umbrellas)
    spread_rows = ones_where(iota((size, torsions), 1) == iota((size, torsions), 0) // umbrellas)
    tile = ones_where(iota((umbrellas, size), 0) == iota((umbrellas, size), 1) % umbrellas)
    tile_rows = ones_where(iota((size, umbrellas), 1) == iota((size, umbrellas), 0) % umbrellas)
    row, column = iota((size, size), 0), iota((size, size), 1)
    torsion = exact_dot(spread_rows, exact_dot(torsion_ref[...].T, spread))
    umbrella = exact_dot(tile_rows, exact_dot(umbrella_ref[...].T, tile))
    return jnp.where(row % umbrellas == column % umbrellas, torsion, 0.0) + jnp.where(
        row // umbrellas == column // umbrellas, umbrella, 0.0
    )


def damping_columns(damping_ref, size):
    slabs, bonds = damping_ref.shape
    bends = size // bonds
    owner = iota((size, bonds), 0) // bends == iota((size, bonds), 1)
    return [
        jnp.sum(
            jnp.where(owner, jnp.broadcast_to(damping_ref[slab : slab + 1, :], (size, bonds)), 0.0),
            axis=1,
            keepdims=True,
        )
        for slab in range(slabs)
    ]


def local_kinetic(fields, high_ref, low_ref, outer, rows):
    outer_high, outer_low = split(outer)
    outer_both = jnp.concatenate([outer_high, outer_high], axis=0)
    parts = [split(field) for field in fields]
    high = jnp.concatenate([part[0] for part in parts], axis=1)
    low = jnp.concatenate([part[1] for part in parts], axis=1)
    both = jnp.concatenate([high, low], axis=1)
    width = high.shape[1]
    lanes = fields[0].shape[1]
    results = []
    for start in range(0, fields[0].shape[0], rows):
        chunk = pl.ds(start, rows)
        product = dot(high_ref[chunk, :], both)
        inner = product[:, :width] + product[:, width:] + dot(low_ref[chunk, :], high)
        line = []
        for at, (part_high, part_low) in enumerate(parts):
            part_high, part_low = part_high[start : start + rows], part_low[start : start + rows]
            turned = dot(jnp.concatenate([part_high, part_low], axis=1), outer_both) + dot(part_high, outer_low)
            line.append(inner[:, at * lanes : (at + 1) * lanes] + turned)
        results.append(line)
    return results


ROWS = 128


def first_kernel(
    prev_ref, curr_ref, potential_ref, damping_ref, bond_ref, bend_ref, torsion_ref, umbrella_ref, message_ref, high_ref, low_ref
):
    slabs, size, lanes = curr_ref.shape
    build_inner(bond_ref, bend_ref, high_ref, low_ref)
    outer = build_outer(torsion_ref, umbrella_ref)
    damping = damping_columns(damping_ref, size)
    stride = 2 * slabs + 1
    fields = [curr_ref[slab] for slab in range(slabs)]
    kinetic = local_kinetic(fields, high_ref, low_ref, outer, ROWS)
    for at, line in enumerate(kinetic):
        start = at * ROWS
        chunk = slice(start, start + ROWS)
        for slab in range(slabs):
            field = fields[slab][chunk]
            total = line[slab] + potential_ref[slab, chunk] * field
            rest = 2.0 * total - damping[slab][chunk] * prev_ref[slab, chunk]
            message_ref[pl.ds(start * stride + slab, ROWS, stride=stride), :] = field
            message_ref[pl.ds(start * stride + slabs + slab, ROWS, stride=stride), :] = rest
        factors = jnp.where(iota((ROWS, lanes), 1) < lanes // 2, damping[0][chunk], damping[1][chunk])
        message_ref[pl.ds(start * stride + 2 * slabs, ROWS, stride=stride), :] = factors


def middle_kernel(slabs, message_ref, radial_ref, twist_ref, back_ref, high_ref, low_ref):
    lanes = message_ref.shape[1]
    radials, twists = radial_ref.shape[0], twist_ref.shape[0]
    groups = radials // slabs
    size = twists * groups
    stride = 2 * slabs + 1

    spread = exact_dot(twist_ref[...], ones_where(iota((twists, size), 0) == iota((twists, size), 1) // groups))
    same_group = iota((groups, size), 0) == iota((groups, size), 1) % groups
    for twist in range(twists):
        block = jnp.where(same_group, jnp.broadcast_to(spread[twist : twist + 1, :], (groups, size)), 0.0)
        high, low = split(block)
        high_ref[pl.ds(twist * groups, groups), :] = high
        low_ref[pl.ds(twist * groups, groups), :] = low

    order = ones_where(iota((radials, radials), 1) == (iota((radials, radials), 0) % groups) * slabs + iota((radials, radials), 0) // groups)
    order_back = ones_where(iota((radials, radials), 0) == (iota((radials, radials), 1) % groups) * slabs + iota((radials, radials), 1) // groups)
    radial_high, radial_low = split(exact_dot(exact_dot(order, radial_ref[...]), order_back))
    radial = jnp.concatenate([radial_high, radial_high, radial_low, radial_low], axis=1)

    def apply(fields):
        parts = [split(field) for field in fields]
        high = jnp.concatenate([part[0] for part in parts], axis=1)
        low = jnp.concatenate([part[1] for part in parts], axis=1)
        both = jnp.concatenate([high, low], axis=1)
        width = high.shape[1]
        outs = [[] for _ in range(slabs)]
        for twist in range(twists):
            rows = slice(twist * groups, (twist + 1) * groups)
            chunk = pl.ds(twist * groups, groups)
            stack = [part[0][rows] for part in parts] + [part[1][rows] for part in parts]
            along = dot(radial, jnp.concatenate(stack + stack, axis=0))
            product = dot(high_ref[chunk, :], both)
            across = product[:, :width] + product[:, width:] + dot(low_ref[chunk, :], high)
            for slab in range(slabs):
                outs[slab].append(along[slab * groups : (slab + 1) * groups] + across[:, slab * lanes : (slab + 1) * lanes])
        return [jnp.concatenate(out, axis=0) for out in outs]

    curr = [message_ref[pl.ds(slab, size, stride=stride), :] for slab in range(slabs)]
    turned = apply(curr)
    factors = message_ref[pl.ds(2 * slabs, size, stride=stride), :]
    following = []
    for slab in range(slabs):
        rest = message_ref[pl.ds(slabs + slab, size, stride=stride), :]
        place = slab * (lanes // 2)
        following.append(factors[:, place : place + 1] * (rest + 2.0 * turned[slab]))
    for slab, value in enumerate(following):
        back_ref[pl.ds(slab, size, stride=2 * slabs), :] = value
    for slab, value in enumerate(apply(following)):
        back_ref[pl.ds(slabs + slab, size, stride=2 * slabs), :] = value


def last_kernel(
    back_ref, curr_ref, potential_ref, damping_ref, bond_ref, bend_ref, torsion_ref, umbrella_ref, next_ref, last_ref, high_ref, low_ref
):
    slabs, size, _ = curr_ref.shape
    build_inner(bond_ref, bend_ref, high_ref, low_ref)
    outer = build_outer(torsion_ref, umbrella_ref)
    damping = damping_columns(damping_ref, size)
    stride = 2 * slabs
    fields = [back_ref[pl.ds(slab, size, stride=stride), :] for slab in range(slabs)]
    for slab in range(slabs):
        next_ref[slab] = fields[slab]
    kinetic = local_kinetic(fields, high_ref, low_ref, outer, ROWS)
    for at, line in enumerate(kinetic):
        start = at * ROWS
        chunk = slice(start, start + ROWS)
        for slab in range(slabs):
            remote = back_ref[pl.ds(start * stride + slabs + slab, ROWS, stride=stride), :]
            total = line[slab] + remote + potential_ref[slab, chunk] * fields[slab][chunk]
            factor = damping[slab][chunk]
            last_ref[slab, chunk] = factor * (2.0 * total - factor * curr_ref[slab, chunk])


PARAMS = pltpu.CompilerParams(vmem_limit_bytes=40 * 1024 * 1024)


def local(
    packet_prev,
    packet_curr,
    potential,
    damping,
    kinetic_radial,
    kinetic_bond,
    kinetic_bend,
    kinetic_twist,
    kinetic_torsion,
    kinetic_umbrella,
):
    slabs, size, _, lanes = packet_curr.shape
    flat = (slabs, size, lanes)
    inner = (kinetic_bond, kinetic_bend, kinetic_torsion, kinetic_umbrella)
    prev, curr, field = (value.reshape(flat) for value in (packet_prev, packet_curr, potential))
    scratch = [pltpu.VMEM((size, size), BF16), pltpu.VMEM((size, size), BF16)]
    stride = 2 * slabs + 1
    message = pl.pallas_call(
        first_kernel,
        out_shape=jax.ShapeDtypeStruct((size * stride, lanes), F32),
        scratch_shapes=scratch,
        compiler_params=PARAMS,
    )(prev, curr, field, damping, *inner)
    message = lax.all_to_all(
        message.reshape(size, stride, 1, lanes), AXES, split_axis=0, concat_axis=0, tiled=True
    ).reshape(size * stride, lanes)
    rows = kinetic_twist.shape[0] * (kinetic_radial.shape[0] // slabs)
    back = pl.pallas_call(
        lambda *refs: middle_kernel(slabs, *refs),
        out_shape=jax.ShapeDtypeStruct((rows * 2 * slabs, lanes), F32),
        scratch_shapes=[pltpu.VMEM((rows, rows), BF16), pltpu.VMEM((rows, rows), BF16)],
        compiler_params=PARAMS,
    )(message, kinetic_radial, kinetic_twist)
    back = lax.all_to_all(
        back.reshape(size, 2 * slabs, lanes), AXES, split_axis=0, concat_axis=0, tiled=True
    ).reshape(size * 2 * slabs, lanes)
    next_term, last_term = pl.pallas_call(
        last_kernel,
        out_shape=(jax.ShapeDtypeStruct(flat, F32), jax.ShapeDtypeStruct(flat, F32)),
        scratch_shapes=scratch,
        compiler_params=PARAMS,
    )(back, curr, field, damping, *inner)
    return next_term.reshape(packet_curr.shape), last_term.reshape(packet_curr.shape)


def solution(mesh):
    placed = (
        P("wide", None, "narrow", None),
        P("wide", None, "narrow", None),
        P("wide", None, "narrow", None),
        P("wide", None),
        P(),
        P(),
        P(),
        P(),
        P(),
        P(),
    )
    return jax.shard_map(
        local,
        mesh=mesh,
        in_specs=placed,
        out_specs=(P("wide", None, "narrow", None), P("wide", None, "narrow", None)),
        check_vma=False,
    )
```

```python
import jax
import jax.numpy as jnp
from jax import lax
from jax.experimental import pallas as pl
from jax.experimental.pallas import tpu as pltpu
from jax.sharding import PartitionSpec as P

AXES = ("wide", "narrow")
F32 = jnp.float32
BF16 = jnp.bfloat16


def exact_dot(left, right):
    return jnp.dot(left, right, precision=lax.Precision.HIGHEST, preferred_element_type=F32)


def dot(left, right):
    return jnp.dot(left, right, preferred_element_type=F32)


def split(value):
    high = value.astype(BF16)
    return high, (value - high.astype(F32)).astype(BF16)


def iota(shape, axis):
    return lax.broadcasted_iota(jnp.int32, shape, axis)


def ones_where(condition):
    return jnp.where(condition, 1.0, 0.0).astype(F32)


def build_inner(bond_ref, bend_ref, high_ref, low_ref):
    bonds, bends = bond_ref.shape[0], bend_ref.shape[0]
    size = bonds * bends
    spread_bond = exact_dot(bond_ref[...], ones_where(iota((bonds, size), 0) == iota((bonds, size), 1) // bends))
    spread_bend = exact_dot(bend_ref[...], ones_where(iota((bends, size), 0) == iota((bends, size), 1) % bends))
    same_bend = iota((bends, size), 0) == iota((bends, size), 1) % bends
    bond_of = iota((bends, size), 1) // bends
    for bond in range(bonds):
        row = jnp.broadcast_to(spread_bond[bond : bond + 1, :], (bends, size))
        block = jnp.where(same_bend, row, 0.0) + jnp.where(bond_of == bond, spread_bend, 0.0)
        high, low = split(block)
        high_ref[pl.ds(bond * bends, bends), :] = high
        low_ref[pl.ds(bond * bends, bends), :] = low


def build_outer(torsion_ref, umbrella_ref):
    torsions, umbrellas = torsion_ref.shape[0], umbrella_ref.shape[0]
    size = torsions * umbrellas
    spread = ones_where(iota((torsions, size), 0) == iota((torsions, size), 1) // umbrellas)
    spread_rows = ones_where(iota((size, torsions), 1) == iota((size, torsions), 0) // umbrellas)
    tile = ones_where(iota((umbrellas, size), 0) == iota((umbrellas, size), 1) % umbrellas)
    tile_rows = ones_where(iota((size, umbrellas), 1) == iota((size, umbrellas), 0) % umbrellas)
    row, column = iota((size, size), 0), iota((size, size), 1)
    torsion = exact_dot(spread_rows, exact_dot(torsion_ref[...].T, spread))
    umbrella = exact_dot(tile_rows, exact_dot(umbrella_ref[...].T, tile))
    return jnp.where(row % umbrellas == column % umbrellas, torsion, 0.0) + jnp.where(
        row // umbrellas == column // umbrellas, umbrella, 0.0
    )


def damping_columns(damping_ref, size):
    slabs, bonds = damping_ref.shape
    bends = size // bonds
    owner = iota((size, bonds), 0) // bends == iota((size, bonds), 1)
    return [
        jnp.sum(
            jnp.where(owner, jnp.broadcast_to(damping_ref[slab : slab + 1, :], (size, bonds)), 0.0),
            axis=1,
            keepdims=True,
        )
        for slab in range(slabs)
    ]


def outer_parts(torsion_ref, umbrella_ref):
    high, low = split(build_outer(torsion_ref, umbrella_ref))
    return jnp.concatenate([high, high], axis=0), low


def outer_parts(torsion_ref, umbrella_ref):
    high, low = split(build_outer(torsion_ref, umbrella_ref))
    return jnp.concatenate([high, high], axis=0), low


def local_kinetic(fields, high_ref, low_ref, outer_both, outer_low, chunk_rows):
    parts = [split(field) for field in fields]
    high = jnp.concatenate([part[0] for part in parts], axis=1)
    both = jnp.concatenate([high] + [part[1] for part in parts], axis=1)
    width = high.shape[1]
    lanes = fields[0].shape[1]
    for start in range(0, fields[0].shape[0], chunk_rows):
        rows = slice(start, start + chunk_rows)
        product = dot(high_ref[rows], both)
        inner = product[:, :width] + product[:, width:] + dot(low_ref[rows], high)
        yield (
            rows,
            [
                inner[:, at * lanes : (at + 1) * lanes]
                + dot(jnp.concatenate([part_high[rows], part_low[rows]], axis=1), outer_both)
                + dot(part_high[rows], outer_low)
                for at, (part_high, part_low) in enumerate(parts)
            ],
        )


CHUNK = 256


def first_kernel(count, *refs):
    sources, result_ref, targets = refs[:count], refs[count], refs[count + 1 : 2 * count + 1]
    message_ref, high_ref, low_ref, arrived, left = refs[2 * count + 1 :]
    copies = [
        pltpu.make_async_copy(source, target, arrived.at[at])
        for at, (source, target) in enumerate(zip(sources, targets))
    ]
    for copy in copies:
        copy.start()
    bond_ref, bend_ref, torsion_ref, umbrella_ref, damping_ref, curr_ref, potential_ref, prev_ref = targets
    slabs, size, lanes = curr_ref.shape
    stride = 2 * slabs + 1
    for copy in copies[:5]:
        copy.wait()
    build_inner(bond_ref, bend_ref, high_ref, low_ref)
    outer_both, outer_low = outer_parts(torsion_ref, umbrella_ref)
    damping = damping_columns(damping_ref, size)
    factors = jnp.where(iota((size, lanes), 1) < lanes // 2, damping[0], damping[1])
    message_ref[pl.ds(2 * slabs, size, stride=stride), :] = factors
    for copy in copies[5:]:
        copy.wait()
    fields = [curr_ref[slab] for slab in range(slabs)]
    for slab in range(slabs):
        message_ref[pl.ds(slab, size, stride=stride), :] = fields[slab]
    sends = []
    for rows, kinetic in local_kinetic(fields, high_ref, low_ref, outer_both, outer_low, CHUNK):
        for slab in range(slabs):
            total = kinetic[slab] + potential_ref[slab, rows] * fields[slab][rows]
            rest = 2.0 * total - damping[slab][rows] * prev_ref[slab, rows]
            message_ref[pl.ds(rows.start * stride + slabs + slab, CHUNK, stride=stride), :] = rest
        part = pl.ds(rows.start * stride, CHUNK * stride)
        sends.append(pltpu.make_async_copy(message_ref.at[part], result_ref.at[part], left.at[len(sends)]))
        sends[-1].start()
    for send in sends:
        send.wait()


def middle_kernel(slabs, message_ref, radial_ref, twist_ref, back_ref, high_ref, low_ref, along_ref, field_ref):
    lanes = message_ref.shape[1]
    radials, twists = radial_ref.shape[0], twist_ref.shape[0]
    groups = radials // slabs
    size = twists * groups
    stride = 2 * slabs + 1
    block = high_ref.shape[0]

    spread = exact_dot(twist_ref[...], ones_where(iota((twists, block), 0) == iota((twists, block), 1) % twists))
    group_of = iota((twists, block), 1) // twists
    spread_high, spread_low = split(spread)
    zero = jnp.zeros_like(spread_high)
    for at in range(block // twists):
        rows = pl.ds(at * twists, twists)
        high_ref[rows, :] = jnp.where(group_of == at, spread_high, zero)
        low_ref[rows, :] = jnp.where(group_of == at, spread_low, zero)

    square = (radials, radials)
    order = ones_where(iota(square, 0) == (iota(square, 1) % groups) * slabs + iota(square, 1) // groups)
    rows = [radial_ref[pl.ds(slab, groups, stride=slabs), :] for slab in range(slabs)]
    radial_high, radial_low = split(exact_dot(jnp.concatenate(rows, axis=0), order))
    radial = jnp.concatenate([radial_high, radial_high, radial_low, radial_low], axis=1)

    def apply(whole, lines):
        for pair in range(0, twists, 2):
            stacks = []
            for twist in (pair, pair + 1):
                parts = [split(lines(slab, twist)) for slab in range(slabs)]
                stack = [part[0] for part in parts] + [part[1] for part in parts]
                stacks.append(jnp.concatenate(stack + stack, axis=0))
            along = dot(radial, jnp.concatenate(stacks, axis=1))
            for at, twist in enumerate((pair, pair + 1)):
                for slab in range(slabs):
                    along_ref[slab, pl.ds(twist, groups, stride=twists), :] = along[
                        slab * groups : (slab + 1) * groups, at * lanes : (at + 1) * lanes
                    ]
        for start in range(0, size, block):
            rows = slice(start, start + block)
            parts = [split(whole(slab)[rows]) for slab in range(slabs)]
            high = jnp.concatenate([part[0] for part in parts], axis=1)
            both = jnp.concatenate([high] + [part[1] for part in parts], axis=1)
            width = high.shape[1]
            product = dot(high_ref[...], both)
            across = product[:, :width] + product[:, width:] + dot(low_ref[...], high)
            yield rows, [along_ref[slab, rows] + across[:, slab * lanes : (slab + 1) * lanes] for slab in range(slabs)]

    def packet(slab):
        return message_ref[pl.ds(slab, size, stride=stride), :]

    def packet_lines(slab, twist):
        return message_ref[pl.ds(twist * stride + slab, groups, stride=twists * stride), :]

    for rows, turned in apply(packet, packet_lines):
        factors = message_ref[pl.ds(rows.start * stride + 2 * slabs, block, stride=stride), :]
        for slab in range(slabs):
            rest = message_ref[pl.ds(rows.start * stride + slabs + slab, block, stride=stride), :]
            place = slab * (lanes // 2)
            following = factors[:, place : place + 1] * (rest + 2.0 * turned[slab])
            field_ref[slab, rows] = following
            back_ref[pl.ds(rows.start * 2 * slabs + slab, block, stride=2 * slabs), :] = following

    def field(slab):
        return field_ref[slab]

    def field_lines(slab, twist):
        return field_ref[slab, pl.ds(twist, groups, stride=twists), :]

    for rows, turned in apply(field, field_lines):
        for slab in range(slabs):
            back_ref[pl.ds(rows.start * 2 * slabs + slabs + slab, block, stride=2 * slabs), :] = turned[slab]


def last_kernel(
    back_ref,
    curr_ref,
    potential_ref,
    damping_ref,
    bond_ref,
    bend_ref,
    torsion_ref,
    umbrella_ref,
    next_ref,
    last_ref,
    high_ref,
    low_ref,
    next_held,
    last_held,
    left,
):
    slabs, size, _ = curr_ref.shape
    stride = 2 * slabs
    fields = [back_ref[pl.ds(slab, size, stride=stride), :] for slab in range(slabs)]
    for slab in range(slabs):
        next_held[slab] = fields[slab]
    sends = [pltpu.make_async_copy(next_held, next_ref, left.at[0])]
    sends[0].start()
    build_inner(bond_ref, bend_ref, high_ref, low_ref)
    outer_both, outer_low = outer_parts(torsion_ref, umbrella_ref)
    damping = damping_columns(damping_ref, size)
    for rows, kinetic in local_kinetic(fields, high_ref, low_ref, outer_both, outer_low, CHUNK):
        for slab in range(slabs):
            remote = back_ref[pl.ds(rows.start * stride + slabs + slab, CHUNK, stride=stride), :]
            total = kinetic[slab] + remote + potential_ref[slab, rows] * fields[slab][rows]
            factor = damping[slab][rows]
            last_held[slab, rows] = factor * (2.0 * total - factor * curr_ref[slab, rows])
            part = pl.ds(rows.start, CHUNK)
            sends.append(
                pltpu.make_async_copy(last_held.at[slab, part], last_ref.at[slab, part], left.at[len(sends)])
            )
            sends[-1].start()
    for send in sends:
        send.wait()


def params(mebibytes):
    return pltpu.CompilerParams(vmem_limit_bytes=mebibytes * 1024 * 1024)


def shaped(*shape, dtype=F32):
    return jax.ShapeDtypeStruct(shape, dtype)


def local(
    packet_prev,
    packet_curr,
    potential,
    damping,
    kinetic_radial,
    kinetic_bond,
    kinetic_bend,
    kinetic_twist,
    kinetic_torsion,
    kinetic_umbrella,
):
    slabs, size, _, lanes = packet_curr.shape
    flat = (slabs, size, lanes)
    inner = (kinetic_bond, kinetic_bend, kinetic_torsion, kinetic_umbrella)
    prev, curr, field = (value.reshape(flat) for value in (packet_prev, packet_curr, potential))
    stride = 2 * slabs + 1
    sources = (*inner, damping, curr, field, prev)
    whole = pl.BlockSpec(memory_space=pltpu.VMEM)
    remote = pl.BlockSpec(memory_space=pltpu.HBM)
    chunks = size // CHUNK
    matrix = [pltpu.VMEM((size, size), BF16)] * 2
    message = pl.pallas_call(
        lambda *refs: first_kernel(len(sources), *refs),
        out_shape=shaped(size * stride, lanes),
        in_specs=[remote] * len(sources),
        out_specs=remote,
        scratch_shapes=[pltpu.VMEM(source.shape, F32) for source in sources]
        + [pltpu.VMEM((size * stride, lanes), F32)]
        + matrix
        + [pltpu.SemaphoreType.DMA((len(sources),)), pltpu.SemaphoreType.DMA((chunks,))],
        compiler_params=params(60),
    )(*sources)
    message = lax.all_to_all(
        message.reshape(size, stride, 1, lanes), AXES, split_axis=0, concat_axis=0, tiled=True
    ).reshape(size * stride, lanes)
    rows = kinetic_twist.shape[0] * (kinetic_radial.shape[0] // slabs)
    block = 256
    back = pl.pallas_call(
        lambda *refs: middle_kernel(slabs, *refs),
        out_shape=shaped(rows * 2 * slabs, lanes),
        scratch_shapes=[pltpu.VMEM((block, block), BF16)] * 2 + [pltpu.VMEM((slabs, rows, lanes), F32)] * 2,
        compiler_params=params(32),
    )(message, kinetic_radial, kinetic_twist)
    back = lax.all_to_all(
        back.reshape(size, 2 * slabs, lanes), AXES, split_axis=0, concat_axis=0, tiled=True
    ).reshape(size * 2 * slabs, lanes)
    next_term, last_term = pl.pallas_call(
        last_kernel,
        out_shape=(shaped(*flat), shaped(*flat)),
        in_specs=[whole] * 8,
        out_specs=(remote, remote),
        scratch_shapes=matrix
        + [pltpu.VMEM(flat, F32)] * 2
        + [pltpu.SemaphoreType.DMA((1 + slabs * chunks,))],
        compiler_params=params(32),
    )(back, curr, field, damping, *inner)
    return next_term.reshape(packet_curr.shape), last_term.reshape(packet_curr.shape)


def solution(mesh):
    placed = (
        P("wide", None, "narrow", None),
        P("wide", None, "narrow", None),
        P("wide", None, "narrow", None),
        P("wide", None),
        P(),
        P(),
        P(),
        P(),
        P(),
        P(),
    )
    return jax.shard_map(
        local,
        mesh=mesh,
        in_specs=placed,
        out_specs=(P("wide", None, "narrow", None), P("wide", None, "narrow", None)),
        check_vma=False,
    )
```

```python
import jax
import jax.numpy as jnp
from jax import lax
from jax.experimental import pallas as pl
from jax.experimental.pallas import tpu as pltpu
from jax.sharding import PartitionSpec as P

AXES = ("wide", "narrow")
F32 = jnp.float32
BF16 = jnp.bfloat16


def exact_dot(left, right):
    return jnp.dot(left, right, precision=lax.Precision.HIGHEST, preferred_element_type=F32)


def dot(left, right):
    return jnp.dot(left, right, preferred_element_type=F32)


def split(value):
    high = value.astype(BF16)
    return high, (value - high.astype(F32)).astype(BF16)


def iota(shape, axis):
    return lax.broadcasted_iota(jnp.int32, shape, axis)


def ones_where(condition):
    return jnp.where(condition, 1.0, 0.0).astype(F32)


def build_inner(bond_ref, bend_ref, high_ref, low_ref):
    bonds, bends = bond_ref.shape[0], bend_ref.shape[0]
    size = bonds * bends
    spread_bond = exact_dot(bond_ref[...], ones_where(iota((bonds, size), 0) == iota((bonds, size), 1) // bends))
    spread_bend = exact_dot(bend_ref[...], ones_where(iota((bends, size), 0) == iota((bends, size), 1) % bends))
    same_bend = iota((bends, size), 0) == iota((bends, size), 1) % bends
    bond_of = iota((bends, size), 1) // bends
    for bond in range(bonds):
        row = jnp.broadcast_to(spread_bond[bond : bond + 1, :], (bends, size))
        block = jnp.where(same_bend, row, 0.0) + jnp.where(bond_of == bond, spread_bend, 0.0)
        high, low = split(block)
        high_ref[pl.ds(bond * bends, bends), :] = high
        low_ref[pl.ds(bond * bends, bends), :] = low


def build_outer(torsion_ref, umbrella_ref, both_ref, low_ref):
    torsions, umbrellas = torsion_ref.shape[0], umbrella_ref.shape[0]
    size = torsions * umbrellas
    place = iota((umbrellas, size), 0)
    column = iota((umbrellas, size), 1)
    spread = exact_dot(torsion_ref[...], ones_where(iota((torsions, size), 0) == iota((torsions, size), 1) // umbrellas))
    tile = exact_dot(umbrella_ref[...], ones_where(place == column % umbrellas))
    blocks = []
    for torsion in range(torsions):
        row = jnp.broadcast_to(spread[torsion : torsion + 1, :], (umbrellas, size))
        blocks.append(
            jnp.where(place == column % umbrellas, row, 0.0) + jnp.where(column // umbrellas == torsion, tile, 0.0)
        )
    high, low = split(jnp.concatenate(blocks, axis=0))
    both_ref[pl.ds(0, size), :] = high
    both_ref[pl.ds(size, size), :] = high
    low_ref[...] = low


def damping_columns(damping_ref, size):
    slabs, bonds = damping_ref.shape
    bends = size // bonds
    owner = iota((size, bonds), 0) // bends == iota((size, bonds), 1)
    return [
        jnp.sum(
            jnp.where(owner, jnp.broadcast_to(damping_ref[slab : slab + 1, :], (size, bonds)), 0.0),
            axis=1,
            keepdims=True,
        )
        for slab in range(slabs)
    ]


def local_kinetic(fields, high_ref, low_ref, both_ref, rest_ref, chunk_rows):
    parts = [split(field) for field in fields]
    high = jnp.concatenate([part[0] for part in parts], axis=1)
    both = jnp.concatenate([high] + [part[1] for part in parts], axis=1)
    width = high.shape[1]
    lanes = fields[0].shape[1]
    for start in range(0, fields[0].shape[0], chunk_rows):
        rows = slice(start, start + chunk_rows)
        product = dot(high_ref[rows], both)
        inner = product[:, :width] + product[:, width:] + dot(low_ref[rows], high)
        yield (
            rows,
            [
                inner[:, at * lanes : (at + 1) * lanes]
                + dot(jnp.concatenate([part_high[rows], part_low[rows]], axis=1), both_ref[...])
                + dot(part_high[rows], rest_ref[...])
                for at, (part_high, part_low) in enumerate(parts)
            ],
        )


CHUNK = 512


def first_kernel(count, *refs):
    sources, results, targets = refs[:count], refs[count : count + 5], refs[count + 5 : 2 * count + 5]
    message_ref, *matrices = results
    arrived = refs[2 * count + 5]
    copies = [
        pltpu.make_async_copy(source, target, arrived.at[at])
        for at, (source, target) in enumerate(zip(sources, targets))
    ]
    for copy in copies:
        copy.start()
    bond_ref, bend_ref, torsion_ref, umbrella_ref, damping_ref, curr_ref, potential_ref, prev_ref = targets
    slabs, size, lanes = curr_ref.shape
    stride = 2 * slabs + 1
    for copy in copies[:5]:
        copy.wait()
    build_outer(torsion_ref, umbrella_ref, *matrices[2:])
    build_inner(bond_ref, bend_ref, *matrices[:2])
    damping = damping_columns(damping_ref, size)
    factors = jnp.where(iota((size, lanes), 1) < lanes // 2, damping[0], damping[1])
    message_ref[pl.ds(2 * slabs, size, stride=stride), :] = factors
    copies[5].wait()
    fields = [curr_ref[slab] for slab in range(slabs)]
    for slab in range(slabs):
        message_ref[pl.ds(slab, size, stride=stride), :] = fields[slab]
    for rows, kinetic in local_kinetic(fields, *matrices, CHUNK):
        if rows.start == 0:
            copies[6].wait()
            copies[7].wait()
        for slab in range(slabs):
            total = kinetic[slab] + potential_ref[slab, rows] * fields[slab][rows]
            rest = 2.0 * total - damping[slab][rows] * prev_ref[slab, rows]
            message_ref[pl.ds(rows.start * stride + slabs + slab, CHUNK, stride=stride), :] = rest


def middle_kernel(slabs, message_ref, radial_ref, twist_ref, back_ref, high_ref, low_ref, along_ref, field_ref):
    lanes = message_ref.shape[1]
    radials, twists = radial_ref.shape[0], twist_ref.shape[0]
    groups = radials // slabs
    size = twists * groups
    stride = 2 * slabs + 1
    block = high_ref.shape[0]

    spread = exact_dot(twist_ref[...], ones_where(iota((twists, block), 0) == iota((twists, block), 1) % twists))
    group_of = iota((twists, block), 1) // twists
    spread_high, spread_low = split(spread)
    zero = jnp.zeros_like(spread_high)
    for at in range(block // twists):
        rows = pl.ds(at * twists, twists)
        high_ref[rows, :] = jnp.where(group_of == at, spread_high, zero)
        low_ref[rows, :] = jnp.where(group_of == at, spread_low, zero)

    square = (radials, radials)
    order = ones_where(iota(square, 0) == (iota(square, 1) % groups) * slabs + iota(square, 1) // groups)
    rows = [radial_ref[pl.ds(slab, groups, stride=slabs), :] for slab in range(slabs)]
    radial_high, radial_low = split(exact_dot(jnp.concatenate(rows, axis=0), order))
    radial = jnp.concatenate([radial_high, radial_high, radial_low], axis=1)

    def apply(whole, lines):
        for pair in range(0, twists, 2):
            stacks = []
            for twist in (pair, pair + 1):
                parts = [split(lines(slab, twist)) for slab in range(slabs)]
                high = [part[0] for part in parts]
                stacks.append(jnp.concatenate(high + [part[1] for part in parts] + high, axis=0))
            along = dot(radial, jnp.concatenate(stacks, axis=1))
            for at, twist in enumerate((pair, pair + 1)):
                for slab in range(slabs):
                    along_ref[slab, pl.ds(twist, groups, stride=twists), :] = along[
                        slab * groups : (slab + 1) * groups, at * lanes : (at + 1) * lanes
                    ]
        for start in range(0, size, block):
            rows = slice(start, start + block)
            parts = [split(whole(slab)[rows]) for slab in range(slabs)]
            high = jnp.concatenate([part[0] for part in parts], axis=1)
            both = jnp.concatenate([high] + [part[1] for part in parts], axis=1)
            width = high.shape[1]
            product = dot(high_ref[...], both)
            across = product[:, :width] + product[:, width:] + dot(low_ref[...], high)
            yield rows, [along_ref[slab, rows] + across[:, slab * lanes : (slab + 1) * lanes] for slab in range(slabs)]

    def packet(slab):
        return message_ref[pl.ds(slab, size, stride=stride), :]

    def packet_lines(slab, twist):
        return message_ref[pl.ds(twist * stride + slab, groups, stride=twists * stride), :]

    for rows, turned in apply(packet, packet_lines):
        factors = message_ref[pl.ds(rows.start * stride + 2 * slabs, block, stride=stride), :]
        for slab in range(slabs):
            rest = message_ref[pl.ds(rows.start * stride + slabs + slab, block, stride=stride), :]
            place = slab * (lanes // 2)
            following = factors[:, place : place + 1] * (rest + 2.0 * turned[slab])
            field_ref[slab, rows] = following
            back_ref[pl.ds(rows.start * 2 * slabs + slab, block, stride=2 * slabs), :] = following

    def field(slab):
        return field_ref[slab]

    def field_lines(slab, twist):
        return field_ref[slab, pl.ds(twist, groups, stride=twists), :]

    for rows, turned in apply(field, field_lines):
        for slab in range(slabs):
            back_ref[pl.ds(rows.start * 2 * slabs + slabs + slab, block, stride=2 * slabs), :] = turned[slab]


def last_kernel(
    back_ref, curr_ref, potential_ref, damping_ref, high_ref, low_ref, both_ref, rest_ref, next_ref, last_ref, next_held, last_held, left
):
    slabs, size, _ = curr_ref.shape
    stride = 2 * slabs
    fields = [back_ref[pl.ds(slab, size, stride=stride), :] for slab in range(slabs)]
    for slab in range(slabs):
        next_held[slab] = fields[slab]
    sends = [pltpu.make_async_copy(next_held, next_ref, left.at[0])]
    sends[0].start()
    damping = damping_columns(damping_ref, size)
    for rows, kinetic in local_kinetic(fields, high_ref, low_ref, both_ref, rest_ref, CHUNK):
        for slab in range(slabs):
            remote = back_ref[pl.ds(rows.start * stride + slabs + slab, CHUNK, stride=stride), :]
            total = kinetic[slab] + remote + potential_ref[slab, rows] * fields[slab][rows]
            factor = damping[slab][rows]
            last_held[slab, rows] = factor * (2.0 * total - factor * curr_ref[slab, rows])
            part = pl.ds(rows.start, CHUNK)
            sends.append(
                pltpu.make_async_copy(last_held.at[slab, part], last_ref.at[slab, part], left.at[len(sends)])
            )
            sends[-1].start()
    for send in sends:
        send.wait()


def params(mebibytes):
    return pltpu.CompilerParams(vmem_limit_bytes=mebibytes * 1024 * 1024)


def shaped(*shape, dtype=F32):
    return jax.ShapeDtypeStruct(shape, dtype)


def local(
    packet_prev,
    packet_curr,
    potential,
    damping,
    kinetic_radial,
    kinetic_bond,
    kinetic_bend,
    kinetic_twist,
    kinetic_torsion,
    kinetic_umbrella,
):
    slabs, size, _, lanes = packet_curr.shape
    flat = (slabs, size, lanes)
    inner = (kinetic_bond, kinetic_bend, kinetic_torsion, kinetic_umbrella)
    prev, curr, field = (value.reshape(flat) for value in (packet_prev, packet_curr, potential))
    stride = 2 * slabs + 1
    sources = tuple(
        pltpu.with_memory_space_constraint(value, pltpu.HBM) for value in (*inner, damping, curr, field, prev)
    )
    whole = pl.BlockSpec(memory_space=pltpu.VMEM)
    remote = pl.BlockSpec(memory_space=pltpu.HBM)
    chunks = size // CHUNK
    message, *matrices = pl.pallas_call(
        lambda *refs: first_kernel(len(sources), *refs),
        out_shape=(
            shaped(size * stride, lanes),
            shaped(size, size, dtype=BF16),
            shaped(size, size, dtype=BF16),
            shaped(2 * lanes, lanes, dtype=BF16),
            shaped(lanes, lanes, dtype=BF16),
        ),
        in_specs=[remote] * len(sources),
        out_specs=[whole] * 5,
        scratch_shapes=[pltpu.VMEM(source.shape, F32) for source in sources]
        + [pltpu.SemaphoreType.DMA((len(sources),))],
        compiler_params=params(32),
    )(*sources)
    message = lax.all_to_all(
        message.reshape(size, stride, 1, lanes), AXES, split_axis=0, concat_axis=0, tiled=True
    ).reshape(size * stride, lanes)
    rows = kinetic_twist.shape[0] * (kinetic_radial.shape[0] // slabs)
    block = 256
    back = pl.pallas_call(
        lambda *refs: middle_kernel(slabs, *refs),
        out_shape=shaped(rows * 2 * slabs, lanes),
        scratch_shapes=[pltpu.VMEM((block, block), BF16)] * 2 + [pltpu.VMEM((slabs, rows, lanes), F32)] * 2,
        compiler_params=params(32),
    )(message, kinetic_radial, kinetic_twist)
    back = lax.all_to_all(
        back.reshape(size, 2 * slabs, lanes), AXES, split_axis=0, concat_axis=0, tiled=True
    ).reshape(size * 2 * slabs, lanes)
    next_term, last_term = pl.pallas_call(
        last_kernel,
        out_shape=(shaped(*flat), shaped(*flat)),
        in_specs=[whole] * 8,
        out_specs=(remote, remote),
        scratch_shapes=[pltpu.VMEM(flat, F32)] * 2 + [pltpu.SemaphoreType.DMA((1 + slabs * chunks,))],
        compiler_params=params(32),
    )(back, curr, field, damping, *matrices)
    return next_term.reshape(packet_curr.shape), last_term.reshape(packet_curr.shape)


def solution(mesh):
    placed = (
        P("wide", None, "narrow", None),
        P("wide", None, "narrow", None),
        P("wide", None, "narrow", None),
        P("wide", None),
        P(),
        P(),
        P(),
        P(),
        P(),
        P(),
    )
    return jax.shard_map(
        local,
        mesh=mesh,
        in_specs=placed,
        out_specs=(P("wide", None, "narrow", None), P("wide", None, "narrow", None)),
        check_vma=False,
    )
```

```python
import jax
import jax.numpy as jnp
from jax import lax
from jax.experimental import pallas as pl
from jax.experimental.pallas import tpu as pltpu
from jax.sharding import PartitionSpec as P

AXES = ("wide", "narrow")
F32 = jnp.float32
BF16 = jnp.bfloat16


def exact_dot(left, right):
    return jnp.dot(left, right, precision=lax.Precision.HIGHEST, preferred_element_type=F32)


def dot(left, right):
    return jnp.dot(left, right, preferred_element_type=F32)


def split(value):
    high = value.astype(BF16)
    return high, (value - high.astype(F32)).astype(BF16)


def iota(shape, axis):
    return lax.broadcasted_iota(jnp.int32, shape, axis)


def ones_where(condition):
    return jnp.where(condition, 1.0, 0.0).astype(F32)


def build_inner(bond_ref, bend_ref, high_ref, low_ref):
    bonds, bends = bond_ref.shape[0], bend_ref.shape[0]
    size = bonds * bends
    spread_bond = exact_dot(bond_ref[...], ones_where(iota((bonds, size), 0) == iota((bonds, size), 1) // bends))
    spread_bend = exact_dot(bend_ref[...], ones_where(iota((bends, size), 0) == iota((bends, size), 1) % bends))
    same_bend = iota((bends, size), 0) == iota((bends, size), 1) % bends
    bond_of = iota((bends, size), 1) // bends
    for bond in range(bonds):
        row = jnp.broadcast_to(spread_bond[bond : bond + 1, :], (bends, size))
        block = jnp.where(same_bend, row, 0.0) + jnp.where(bond_of == bond, spread_bend, 0.0)
        high, low = split(block)
        high_ref[pl.ds(bond * bends, bends), :] = high
        low_ref[pl.ds(bond * bends, bends), :] = low


def build_outer(torsion_ref, umbrella_ref, both_ref, low_ref):
    torsions, umbrellas = torsion_ref.shape[0], umbrella_ref.shape[0]
    size = torsions * umbrellas
    place = iota((umbrellas, size), 0)
    column = iota((umbrellas, size), 1)
    spread = exact_dot(torsion_ref[...], ones_where(iota((torsions, size), 0) == iota((torsions, size), 1) // umbrellas))
    tile = exact_dot(umbrella_ref[...], ones_where(place == column % umbrellas))
    blocks = []
    for torsion in range(torsions):
        row = jnp.broadcast_to(spread[torsion : torsion + 1, :], (umbrellas, size))
        blocks.append(
            jnp.where(place == column % umbrellas, row, 0.0) + jnp.where(column // umbrellas == torsion, tile, 0.0)
        )
    high, low = split(jnp.concatenate(blocks, axis=0))
    both_ref[pl.ds(0, size), :] = high
    both_ref[pl.ds(size, size), :] = high
    low_ref[...] = low


def damping_columns(damping_ref, size):
    slabs, bonds = damping_ref.shape
    bends = size // bonds
    owner = iota((size, bonds), 0) // bends == iota((size, bonds), 1)
    return [
        jnp.sum(
            jnp.where(owner, jnp.broadcast_to(damping_ref[slab : slab + 1, :], (size, bonds)), 0.0),
            axis=1,
            keepdims=True,
        )
        for slab in range(slabs)
    ]


def local_kinetic(fields, high_ref, low_ref, both_ref, rest_ref, chunk_rows):
    parts = [split(field) for field in fields]
    high = jnp.concatenate([part[0] for part in parts], axis=1)
    both = jnp.concatenate([high] + [part[1] for part in parts], axis=1)
    width = high.shape[1]
    lanes = fields[0].shape[1]
    for start in range(0, fields[0].shape[0], chunk_rows):
        rows = slice(start, start + chunk_rows)
        product = dot(high_ref[rows], both)
        inner = product[:, :width] + product[:, width:] + dot(low_ref[rows], high)
        yield (
            rows,
            [
                inner[:, at * lanes : (at + 1) * lanes]
                + dot(jnp.concatenate([part_high[rows], part_low[rows]], axis=1), both_ref[...])
                + dot(part_high[rows], rest_ref[...])
                for at, (part_high, part_low) in enumerate(parts)
            ],
        )


LAST_CHUNK = 256


def first_kernel(count, *refs):
    sources, results, targets = refs[:count], refs[count : count + 5], refs[count + 5 : 2 * count + 5]
    message_ref, *matrices = results
    arrived = refs[2 * count + 5]
    copies = [
        pltpu.make_async_copy(source, target, arrived.at[at])
        for at, (source, target) in enumerate(zip(sources, targets))
    ]
    for copy in copies:
        copy.start()
    bond_ref, bend_ref, torsion_ref, umbrella_ref, damping_ref, curr_ref, potential_ref, prev_ref = targets
    slabs, size, lanes = curr_ref.shape
    stride = 2 * slabs + 1
    for copy in copies[:5]:
        copy.wait()
    build_outer(torsion_ref, umbrella_ref, *matrices[2:])
    build_inner(bond_ref, bend_ref, *matrices[:2])
    damping = damping_columns(damping_ref, size)
    factors = jnp.where(iota((size, lanes), 1) < lanes // 2, damping[0], damping[1])
    message_ref[pl.ds(2 * slabs, size, stride=stride), :] = factors
    copies[5].wait()
    fields = [curr_ref[slab] for slab in range(slabs)]
    for slab in range(slabs):
        message_ref[pl.ds(slab, size, stride=stride), :] = fields[slab]
    for rows, kinetic in local_kinetic(fields, *matrices, size):
        if rows.start == 0:
            copies[6].wait()
            copies[7].wait()
        for slab in range(slabs):
            total = kinetic[slab] + potential_ref[slab, rows] * fields[slab][rows]
            rest = 2.0 * total - damping[slab][rows] * prev_ref[slab, rows]
            message_ref[pl.ds(slabs + slab, size, stride=stride), :] = rest


CORES = 2


def return_order(wide, narrow):
    return [(chip * CORES + core) * narrow + at for chip in range(wide // CORES) for at in range(narrow) for core in range(CORES)]


def return_rows(peer, run, width, first):
    chip, core = divmod(peer // run, CORES)
    return pl.ds((chip * CORES * run + core) * width + first, run, stride=CORES * width)


def square_of_parts(high, low):
    return jnp.concatenate([jnp.concatenate([high, high], axis=1), jnp.concatenate([low, low], axis=1)], axis=0)


def middle_kernel(slabs, message_ref, radial_ref, twist_ref, back_ref, along_ref, field_ref):
    lanes = message_ref.shape[1]
    radials, twists = radial_ref.shape[0], twist_ref.shape[0]
    groups = radials // slabs
    size = twists * groups
    stride = 2 * slabs + 1
    block = 128

    spread = exact_dot(twist_ref[...], ones_where(iota((twists, block), 0) == iota((twists, block), 1) % twists))
    group_of = iota((twists, block), 1) // twists
    twist_high, twist_low = split(
        jnp.concatenate([jnp.where(group_of == at, spread, 0.0) for at in range(block // twists)], axis=0)
    )
    twist_square = square_of_parts(twist_high, twist_low)

    square = (radials, radials)
    order = ones_where(iota(square, 0) == (iota(square, 1) % groups) * slabs + iota(square, 1) // groups)
    rows = [radial_ref[pl.ds(slab, groups, stride=slabs), :] for slab in range(slabs)]
    radial_high, radial_low = split(exact_dot(jnp.concatenate(rows, axis=0), order))
    radial = square_of_parts(radial_high, radial_low)

    def apply(whole, lines):
        for pair in range(0, twists, 2):
            stacks = []
            for twist in (pair, pair + 1):
                parts = [split(lines(slab, twist)) for slab in range(slabs)]
                stacks.append(jnp.concatenate([part[0] for part in parts] + [part[1] for part in parts], axis=0))
            along = dot(radial, jnp.concatenate(stacks, axis=1))
            along = along[:radials] + along[radials:]
            for at, twist in enumerate((pair, pair + 1)):
                for slab in range(slabs):
                    along_ref[slab, pl.ds(twist, groups, stride=twists), :] = along[
                        slab * groups : (slab + 1) * groups, at * lanes : (at + 1) * lanes
                    ]
        for start in range(0, size, block):
            rows = slice(start, start + block)
            parts = [split(whole(slab)[rows]) for slab in range(slabs)]
            both = [jnp.concatenate([part[at] for part in parts], axis=1) for at in range(2)]
            across = dot(twist_square, jnp.concatenate(both, axis=0))
            across = across[:block] + across[block:]
            yield rows, [along_ref[slab, rows] + across[:, slab * lanes : (slab + 1) * lanes] for slab in range(slabs)]

    def send(value, start, first):
        for at in range(0, block, twists):
            back_ref[return_rows(start + at, twists, 2 * slabs, first), :] = value[at : at + twists]

    def packet(slab):
        return message_ref[pl.ds(slab, size, stride=stride), :]

    def packet_lines(slab, twist):
        return message_ref[pl.ds(twist * stride + slab, groups, stride=twists * stride), :]

    for rows, turned in apply(packet, packet_lines):
        factors = message_ref[pl.ds(rows.start * stride + 2 * slabs, block, stride=stride), :]
        for slab in range(slabs):
            rest = message_ref[pl.ds(rows.start * stride + slabs + slab, block, stride=stride), :]
            place = slab * (lanes // 2)
            following = factors[:, place : place + 1] * (rest + 2.0 * turned[slab])
            field_ref[slab, rows] = following
            send(following, rows.start, slab)

    def field(slab):
        return field_ref[slab]

    def field_lines(slab, twist):
        return field_ref[slab, pl.ds(twist, groups, stride=twists), :]

    for rows, turned in apply(field, field_lines):
        for slab in range(slabs):
            send(turned[slab], rows.start, slabs + slab)


def last_kernel(
    run,
    back_ref,
    curr_ref,
    potential_ref,
    damping_ref,
    high_ref,
    low_ref,
    both_ref,
    rest_ref,
    next_ref,
    last_ref,
    next_held,
    last_held,
    left,
):
    slabs, size, _ = curr_ref.shape

    def received(start, rows, first):
        pieces = [back_ref[return_rows(peer, run, 2 * slabs, first), :] for peer in range(start, start + rows, run)]
        return jnp.concatenate(pieces, axis=0)

    fields = [received(0, size, slab) for slab in range(slabs)]
    for slab in range(slabs):
        next_held[slab] = fields[slab]
    sends = [pltpu.make_async_copy(next_held, next_ref, left.at[0])]
    sends[0].start()
    damping = damping_columns(damping_ref, size)
    for rows, kinetic in local_kinetic(fields, high_ref, low_ref, both_ref, rest_ref, LAST_CHUNK):
        for slab in range(slabs):
            remote = received(rows.start, LAST_CHUNK, slabs + slab)
            total = kinetic[slab] + remote + potential_ref[slab, rows] * fields[slab][rows]
            factor = damping[slab][rows]
            last_held[slab, rows] = factor * (2.0 * total - factor * curr_ref[slab, rows])
            part = pl.ds(rows.start, LAST_CHUNK)
            sends.append(
                pltpu.make_async_copy(last_held.at[slab, part], last_ref.at[slab, part], left.at[len(sends)])
            )
            sends[-1].start()
    for send in sends:
        send.wait()


def params(mebibytes):
    return pltpu.CompilerParams(vmem_limit_bytes=mebibytes * 1024 * 1024)


def shaped(*shape, dtype=F32):
    return jax.ShapeDtypeStruct(shape, dtype)


def local(
    packet_prev,
    packet_curr,
    potential,
    damping,
    kinetic_radial,
    kinetic_bond,
    kinetic_bend,
    kinetic_twist,
    kinetic_torsion,
    kinetic_umbrella,
):
    slabs, size, _, lanes = packet_curr.shape
    narrow = lax.axis_size("narrow")
    flat = (slabs, size, lanes)
    inner = (kinetic_bond, kinetic_bend, kinetic_torsion, kinetic_umbrella)
    prev, curr, field = (value.reshape(flat) for value in (packet_prev, packet_curr, potential))
    stride = 2 * slabs + 1
    sources = tuple(
        pltpu.with_memory_space_constraint(value, pltpu.HBM) for value in (*inner, damping, curr, field, prev)
    )
    whole = pl.BlockSpec(memory_space=pltpu.VMEM)
    remote = pl.BlockSpec(memory_space=pltpu.HBM)
    chunks = size // LAST_CHUNK
    message, *matrices = pl.pallas_call(
        lambda *refs: first_kernel(len(sources), *refs),
        out_shape=(
            shaped(size * stride, lanes),
            shaped(size, size, dtype=BF16),
            shaped(size, size, dtype=BF16),
            shaped(2 * lanes, lanes, dtype=BF16),
            shaped(lanes, lanes, dtype=BF16),
        ),
        in_specs=[remote] * len(sources),
        out_specs=[whole] * 5,
        scratch_shapes=[pltpu.VMEM(source.shape, F32) for source in sources]
        + [pltpu.SemaphoreType.DMA((len(sources),))],
        compiler_params=params(32),
    )(*sources)
    message = lax.all_to_all(
        message.reshape(size, stride, 1, lanes), AXES, split_axis=0, concat_axis=0, tiled=True
    ).reshape(size * stride, lanes)
    rows = kinetic_twist.shape[0] * (kinetic_radial.shape[0] // slabs)
    back = pl.pallas_call(
        lambda *refs: middle_kernel(slabs, *refs),
        out_shape=shaped(rows * 2 * slabs, lanes),
        scratch_shapes=[pltpu.VMEM((slabs, rows, lanes), F32)] * 2,
        compiler_params=params(32),
    )(message, kinetic_radial, kinetic_twist)
    back = lax.all_to_all(
        back.reshape(size, 2 * slabs, lanes),
        AXES,
        split_axis=0,
        concat_axis=0,
        tiled=True,
        axis_index_groups=[return_order(lax.axis_size("wide"), narrow)],
    ).reshape(size * 2 * slabs, lanes)
    next_term, last_term = pl.pallas_call(
        lambda *refs: last_kernel(narrow, *refs),
        out_shape=(shaped(*flat), shaped(*flat)),
        in_specs=[whole] * 8,
        out_specs=(remote, remote),
        scratch_shapes=[pltpu.VMEM(flat, F32)] * 2 + [pltpu.SemaphoreType.DMA((1 + slabs * chunks,))],
        compiler_params=params(32),
    )(back, curr, field, damping, *matrices)
    return next_term.reshape(packet_curr.shape), last_term.reshape(packet_curr.shape)


def solution(mesh):
    placed = (
        P("wide", None, "narrow", None),
        P("wide", None, "narrow", None),
        P("wide", None, "narrow", None),
        P("wide", None),
        P(),
        P(),
        P(),
        P(),
        P(),
        P(),
    )
    return jax.shard_map(
        local,
        mesh=mesh,
        in_specs=placed,
        out_specs=(P("wide", None, "narrow", None), P("wide", None, "narrow", None)),
        check_vma=False,
    )
```

```python
import jax
import jax.numpy as jnp
from jax import lax
from jax.experimental import pallas as pl
from jax.experimental.pallas import tpu as pltpu
from jax.sharding import PartitionSpec as P

AXES = ("wide", "narrow")
F32 = jnp.float32
BF16 = jnp.bfloat16


def exact_dot(left, right):
    return jnp.dot(left, right, precision=lax.Precision.HIGHEST, preferred_element_type=F32)


def dot(left, right):
    return jnp.dot(left, right, preferred_element_type=F32)


def split(value):
    high = value.astype(BF16)
    return high, (value - high.astype(F32)).astype(BF16)


def iota(shape, axis):
    return lax.broadcasted_iota(jnp.int32, shape, axis)


def ones_where(condition):
    return jnp.where(condition, 1.0, 0.0).astype(F32)


def square_of_parts(high, low):
    return jnp.concatenate([jnp.concatenate([high, high], axis=1), jnp.concatenate([low, low], axis=1)], axis=0)


def repeated(matrix_ref, copies):
    count = matrix_ref.shape[0]
    size = count * copies
    spread = exact_dot(matrix_ref[...], ones_where(iota((count, size), 0) == iota((count, size), 1) % count))
    copy_of = iota((count, size), 1) // count
    return jnp.concatenate([jnp.where(copy_of == at, spread, 0.0) for at in range(copies)], axis=0)


def build_outer(torsion_ref, umbrella_ref):
    torsions, umbrellas = torsion_ref.shape[0], umbrella_ref.shape[0]
    size = torsions * umbrellas
    place = iota((umbrellas, size), 0)
    column = iota((umbrellas, size), 1)
    spread = exact_dot(torsion_ref[...], ones_where(iota((torsions, size), 0) == iota((torsions, size), 1) // umbrellas))
    tile = exact_dot(umbrella_ref[...], ones_where(place == column % umbrellas))
    blocks = []
    for torsion in range(torsions):
        row = jnp.broadcast_to(spread[torsion : torsion + 1, :], (umbrellas, size))
        blocks.append(
            jnp.where(place == column % umbrellas, row, 0.0) + jnp.where(column // umbrellas == torsion, tile, 0.0)
        )
    high, low = split(jnp.concatenate(blocks, axis=0))
    both = jnp.concatenate([high, low], axis=1)
    return jnp.concatenate([both, both], axis=0)


BLOCK = 128


def build_local(bond_ref, bend_ref, torsion_ref, umbrella_ref):
    bends = bend_ref.shape[0]
    return (
        square_of_parts(*split(bond_ref[...])),
        square_of_parts(*split(repeated(bend_ref, BLOCK // bends))),
        build_outer(torsion_ref, umbrella_ref),
    )


def damping_columns(damping_ref, size):
    slabs, bonds = damping_ref.shape
    bends = size // bonds
    owner = iota((size, bonds), 0) // bends == iota((size, bonds), 1)
    return [
        jnp.sum(
            jnp.where(owner, jnp.broadcast_to(damping_ref[slab : slab + 1, :], (size, bonds)), 0.0),
            axis=1,
            keepdims=True,
        )
        for slab in range(slabs)
    ]


def local_kinetic(field_ref, bond_ref, bond_square, bend_square, outer_square):
    slabs, size, lanes = field_ref.shape
    bonds = bond_square.shape[0] // 2
    bends = size // bonds
    for bend in range(bends):
        lines = pl.ds(bend, bonds, stride=bends)
        parts = [split(field_ref[slab, lines, :]) for slab in range(slabs)]
        both = [jnp.concatenate([part[at] for part in parts], axis=1) for at in range(2)]
        along = dot(bond_square, jnp.concatenate(both, axis=0))
        along = along[:bonds] + along[bonds:]
        for slab in range(slabs):
            bond_ref[slab, lines, :] = along[:, slab * lanes : (slab + 1) * lanes]
    for start in range(0, size, BLOCK):
        rows = slice(start, start + BLOCK)
        parts = [split(field_ref[slab, rows]) for slab in range(slabs)]
        both = [jnp.concatenate([part[at] for part in parts], axis=1) for at in range(2)]
        across = dot(bend_square, jnp.concatenate(both, axis=0))
        across = across[:BLOCK] + across[BLOCK:]
        totals = []
        for slab in range(slabs):
            turned = dot(jnp.concatenate(parts[slab], axis=1), outer_square)
            totals.append(
                bond_ref[slab, rows]
                + across[:, slab * lanes : (slab + 1) * lanes]
                + (turned[:, :lanes] + turned[:, lanes:])
            )
        yield rows, totals


def first_kernel(count, *refs):
    sources, message_ref, targets = refs[:count], refs[count], refs[count + 1 : 2 * count + 1]
    along_ref, arrived = refs[2 * count + 1 :]
    copies = [
        pltpu.make_async_copy(source, target, arrived.at[at])
        for at, (source, target) in enumerate(zip(sources, targets))
    ]
    for copy in copies:
        copy.start()
    bond_ref, bend_ref, torsion_ref, umbrella_ref, damping_ref, curr_ref, potential_ref, prev_ref = targets
    slabs, size, lanes = curr_ref.shape
    stride = 2 * slabs + 1
    for copy in copies[:5]:
        copy.wait()
    matrices = build_local(bond_ref, bend_ref, torsion_ref, umbrella_ref)
    damping = damping_columns(damping_ref, size)
    factors = jnp.where(iota((size, lanes), 1) < lanes // 2, damping[0], damping[1])
    message_ref[pl.ds(2 * slabs, size, stride=stride), :] = factors
    copies[5].wait()
    for slab in range(slabs):
        message_ref[pl.ds(slab, size, stride=stride), :] = curr_ref[slab]
    for rows, kinetic in local_kinetic(curr_ref, along_ref, *matrices):
        if rows.start == 0:
            copies[6].wait()
            copies[7].wait()
        for slab in range(slabs):
            total = kinetic[slab] + potential_ref[slab, rows] * curr_ref[slab, rows]
            rest = 2.0 * total - damping[slab][rows] * prev_ref[slab, rows]
            message_ref[pl.ds(rows.start * stride + slabs + slab, BLOCK, stride=stride), :] = rest


CORES = 2
HALVES = 2


def place_of(chip, chips):
    level, half = divmod(chip, HALVES)
    return (half + 1) * (chips // HALVES) - 1 - level


def return_order(wide, narrow):
    chips = wide // CORES
    return [
        (chip * CORES + core) * narrow + at
        for chip in sorted(range(chips), key=lambda chip: place_of(chip, chips))
        for at in range(narrow)
        for core in range(CORES)
    ]


def return_rows(peer, run, size, width, first):
    chip, core = divmod(peer // run, CORES)
    place = place_of(chip, size // (CORES * run))
    return pl.ds((place * CORES * run + core) * width + first, run, stride=CORES * width)


def middle_kernel(slabs, message_ref, radial_ref, twist_ref, back_ref, along_ref, field_ref):
    lanes = message_ref.shape[1]
    radials, twists = radial_ref.shape[0], twist_ref.shape[0]
    groups = radials // slabs
    size = twists * groups
    stride = 2 * slabs + 1
    block = BLOCK

    twist_square = square_of_parts(*split(repeated(twist_ref, BLOCK // twists)))

    square = (radials, radials)
    order = ones_where(iota(square, 0) == (iota(square, 1) % groups) * slabs + iota(square, 1) // groups)
    rows = [radial_ref[pl.ds(slab, groups, stride=slabs), :] for slab in range(slabs)]
    radial_high, radial_low = split(exact_dot(jnp.concatenate(rows, axis=0), order))
    radial = square_of_parts(radial_high, radial_low)

    def apply(whole, lines):
        for pair in range(0, twists, 2):
            stacks = []
            for twist in (pair, pair + 1):
                parts = [split(lines(slab, twist)) for slab in range(slabs)]
                stacks.append(jnp.concatenate([part[0] for part in parts] + [part[1] for part in parts], axis=0))
            along = dot(radial, jnp.concatenate(stacks, axis=1))
            along = along[:radials] + along[radials:]
            for at, twist in enumerate((pair, pair + 1)):
                for slab in range(slabs):
                    along_ref[slab, pl.ds(twist, groups, stride=twists), :] = along[
                        slab * groups : (slab + 1) * groups, at * lanes : (at + 1) * lanes
                    ]
        for start in range(0, size, block):
            rows = slice(start, start + block)
            parts = [split(whole(slab)[rows]) for slab in range(slabs)]
            both = [jnp.concatenate([part[at] for part in parts], axis=1) for at in range(2)]
            across = dot(twist_square, jnp.concatenate(both, axis=0))
            across = across[:block] + across[block:]
            yield rows, [along_ref[slab, rows] + across[:, slab * lanes : (slab + 1) * lanes] for slab in range(slabs)]

    def send(value, start, first):
        for at in range(0, block, twists):
            back_ref[return_rows(start + at, twists, size, 2 * slabs, first), :] = value[at : at + twists]

    def packet(slab):
        return message_ref[pl.ds(slab, size, stride=stride), :]

    def packet_lines(slab, twist):
        return message_ref[pl.ds(twist * stride + slab, groups, stride=twists * stride), :]

    for rows, turned in apply(packet, packet_lines):
        factors = message_ref[pl.ds(rows.start * stride + 2 * slabs, block, stride=stride), :]
        for slab in range(slabs):
            rest = message_ref[pl.ds(rows.start * stride + slabs + slab, block, stride=stride), :]
            place = slab * (lanes // 2)
            following = factors[:, place : place + 1] * (rest + 2.0 * turned[slab])
            field_ref[slab, rows] = following
            send(following, rows.start, slab)

    def field(slab):
        return field_ref[slab]

    def field_lines(slab, twist):
        return field_ref[slab, pl.ds(twist, groups, stride=twists), :]

    for rows, turned in apply(field, field_lines):
        for slab in range(slabs):
            send(turned[slab], rows.start, slabs + slab)


def last_kernel(
    run,
    back_ref,
    curr_ref,
    potential_ref,
    damping_ref,
    bond_ref,
    bend_ref,
    torsion_ref,
    umbrella_ref,
    next_ref,
    last_ref,
    next_held,
    last_held,
    along_ref,
    left,
):
    slabs, size, _ = curr_ref.shape

    def received(start, rows, first):
        peers = range(start, start + rows, run)
        return jnp.concatenate([back_ref[return_rows(peer, run, size, 2 * slabs, first), :] for peer in peers], axis=0)

    for slab in range(slabs):
        next_held[slab] = received(0, size, slab)
    sends = [pltpu.make_async_copy(next_held, next_ref, left.at[0])]
    sends[0].start()
    damping = damping_columns(damping_ref, size)
    matrices = build_local(bond_ref, bend_ref, torsion_ref, umbrella_ref)
    for rows, kinetic in local_kinetic(next_held, along_ref, *matrices):
        for slab in range(slabs):
            remote = received(rows.start, BLOCK, slabs + slab)
            total = kinetic[slab] + remote + potential_ref[slab, rows] * next_held[slab, rows]
            factor = damping[slab][rows]
            last_held[slab, rows] = factor * (2.0 * total - factor * curr_ref[slab, rows])
        part = pl.ds(rows.start, BLOCK)
        sends.append(
            pltpu.make_async_copy(last_held.at[:, part], last_ref.at[:, part], left.at[len(sends)])
        )
        sends[-1].start()
    for send in sends:
        send.wait()


def params(mebibytes):
    return pltpu.CompilerParams(vmem_limit_bytes=mebibytes * 1024 * 1024)


def shaped(*shape, dtype=F32):
    return jax.ShapeDtypeStruct(shape, dtype)


def local(
    packet_prev,
    packet_curr,
    potential,
    damping,
    kinetic_radial,
    kinetic_bond,
    kinetic_bend,
    kinetic_twist,
    kinetic_torsion,
    kinetic_umbrella,
):
    slabs, size, _, lanes = packet_curr.shape
    narrow = lax.axis_size("narrow")
    flat = (slabs, size, lanes)
    inner = (kinetic_bond, kinetic_bend, kinetic_torsion, kinetic_umbrella)
    prev, curr, field = (value.reshape(flat) for value in (packet_prev, packet_curr, potential))
    stride = 2 * slabs + 1
    sources = tuple(
        pltpu.with_memory_space_constraint(value, pltpu.HBM) for value in (*inner, damping, curr, field, prev)
    )
    whole = pl.BlockSpec(memory_space=pltpu.VMEM)
    remote = pl.BlockSpec(memory_space=pltpu.HBM)
    held = pltpu.VMEM(flat, F32)
    message = pl.pallas_call(
        lambda *refs: first_kernel(len(sources), *refs),
        out_shape=shaped(size * stride, lanes),
        in_specs=[remote] * len(sources),
        out_specs=whole,
        scratch_shapes=[pltpu.VMEM(source.shape, F32) for source in sources]
        + [held, pltpu.SemaphoreType.DMA((len(sources),))],
        compiler_params=params(32),
    )(*sources)
    message = lax.all_to_all(
        message.reshape(size, stride, 1, lanes), AXES, split_axis=0, concat_axis=0, tiled=True
    ).reshape(size * stride, lanes)
    rows = kinetic_twist.shape[0] * (kinetic_radial.shape[0] // slabs)
    back = pl.pallas_call(
        lambda *refs: middle_kernel(slabs, *refs),
        out_shape=shaped(rows * 2 * slabs, lanes),
        scratch_shapes=[pltpu.VMEM((slabs, rows, lanes), F32)] * 2,
        compiler_params=params(32),
    )(message, kinetic_radial, kinetic_twist)
    back = lax.all_to_all(
        back.reshape(size, 2 * slabs, lanes),
        AXES,
        split_axis=0,
        concat_axis=0,
        tiled=True,
        axis_index_groups=[return_order(lax.axis_size("wide"), narrow)],
    ).reshape(size * 2 * slabs, lanes)
    next_term, last_term = pl.pallas_call(
        lambda *refs: last_kernel(narrow, *refs),
        out_shape=(shaped(*flat), shaped(*flat)),
        in_specs=[whole] * 8,
        out_specs=(remote, remote),
        scratch_shapes=[held] * 3 + [pltpu.SemaphoreType.DMA((1 + slabs * (size // BLOCK),))],
        compiler_params=params(32),
    )(back, curr, field, damping, *inner)
    return next_term.reshape(packet_curr.shape), last_term.reshape(packet_curr.shape)


def solution(mesh):
    placed = (
        P("wide", None, "narrow", None),
        P("wide", None, "narrow", None),
        P("wide", None, "narrow", None),
        P("wide", None),
        P(),
        P(),
        P(),
        P(),
        P(),
        P(),
    )
    return jax.shard_map(
        local,
        mesh=mesh,
        in_specs=placed,
        out_specs=(P("wide", None, "narrow", None), P("wide", None, "narrow", None)),
        check_vma=False,
    )
```
